32 devices in a mesh: rows: 8 (over z, y), cols: 4 (over x, core).
Axes of the slice: x: 2, y: 2, z: 4, core: 2. Of those that a mesh axis runs over, the one named last changes fastest.
Arguments:
- images: bfloat16 [64, 360, 128], P('rows'), may hold values from -8 to 8
- partners: int32 [8, 8], P('rows'), may hold values from 0 to 7, each once within a row
- counts: int32 [8], P('rows'), may hold values from 1 to 8
- start: float32 [8, 24], P('rows'), may hold values from -6 to 6
Outputs:
- first_vec: float32 [8, 24], P('rows')
- second_vec: float32 [8, 24], P('rows')
The draws below stay inside these ranges and needn't reach their ends.
Inputs may be any that keep to these rules, and one draw needn't show every extreme that they name: Each row of partners lists every code of 0 to 7 once; only its first counts[I] entries are pairs.
All inputs are finite; a program needn't handle non-finite values.
Results may differ from the reference program's by a relative error of at most 0.0003.
Values may be sent and summed in bfloat16 or wider, within the bound.
A program may use at most 64 MiB of HBM per device.

```python
import math
import jax
import jax.numpy as jnp
from jax import lax

LINES = 360
RADII = 128
IMG_BLK = 8
NBLK = 8
SLOTS = 8
HALO = 4
IMAGES = 64
VEC = 24


def draw_images(key, part):
    key_noise = jax.random.fold_in(key, 0)
    noise = jax.random.normal(key_noise, (IMAGES, LINES, RADII), jnp.float32)
    values = noise
    return jnp.clip(values, -8.0, 8.0).astype(jnp.bfloat16)


def draw_start(key, part):
    key_values = jax.random.fold_in(key, 0)
    values = jnp.clip(jax.random.normal(key_values, (NBLK, VEC), jnp.float32), -6.0, 6.0)
    return values.astype(jnp.float32)


def plant(array, rng, low, high):
    longest = array.shape.index(max(array.shape))
    spots = []
    for shift in (0, 1):
        where = [jax.random.randint(jax.random.fold_in(rng, axis), (), 0, length) for axis, length in enumerate(array.shape)]
        where[longest] = (where[longest] + shift) % array.shape[longest]
        spots.append(tuple(where))
    return array.at[spots[0]].set(low).at[spots[1]].set(high)


def setup_inputs(seed: int = 0) -> dict:
    arg_keys = jax.random.split(jax.random.key(seed), 5)
    return {
        "images": draw_images(jax.random.fold_in(arg_keys[4], 71), 0),
        "partners": jax.vmap(lambda own: jax.random.permutation(own, SLOTS))(jax.random.split(arg_keys[1], NBLK)).reshape((NBLK, SLOTS)).astype(jnp.int32),
        "counts": plant(jax.random.randint(arg_keys[2], (NBLK,), 1, SLOTS + 1), jax.random.fold_in(arg_keys[2], 1), 1, SLOTS).astype(jnp.int32),
        "start": draw_start(jax.random.fold_in(arg_keys[4], 71), 0),
    }


score_gain = 0.4
norm_eps = 1e-06

def line_table(lines):
    angle = 2.0 * math.pi * jnp.arange(lines).astype(jnp.float32) / lines
    return jnp.stack([jnp.cos(angle), jnp.sin(angle), jnp.cos(2.0 * angle)], axis=1)

def pair_tile(own, other, table):
    count, lines, radii = own.shape
    others = other.shape[0]
    flat = other.reshape(others * lines, radii)

    def one_image(lines_a):
        scores = lax.dot_general(lines_a, flat, (((1,), (1,)), ((), ())), preferred_element_type=jnp.float32) * score_gain
        shaped = scores.reshape(lines, others, lines)
        top = lax.optimization_barrier(jnp.max(shaped, axis=(0, 2)))
        weights = jnp.exp(shaped - top[None, :, None])
        total = lax.optimization_barrier(jnp.sum(weights, axis=(0, 2)))
        left = jnp.einsum('lp,lbk->pbk', table, weights, precision=lax.Precision.HIGHEST)
        rel = jnp.einsum('pbk,kq->pbq', left, table, precision=lax.Precision.HIGHEST)
        return rel / total[None, :, None]
    stacked = lax.map(one_image, own)
    return jnp.transpose(stacked, (1, 0, 3, 2)).reshape(3 * count, 3 * others)

def offsets_of(codes, halo):
    return jnp.where(codes < halo, codes - halo, codes - halo + 1).astype(jnp.int32)

def reference(images, partners, counts, start):
    blocks = images.reshape(NBLK, IMG_BLK, LINES, RADII)
    table = line_table(LINES)
    block_ids = jnp.arange(NBLK).astype(jnp.int32)
    partner_ids = (block_ids[:, None] + offsets_of(partners, HALO)) % NBLK
    valid = jnp.arange(SLOTS).astype(jnp.int32)[None, :] < counts[:, None]

    def row_tiles(index):
        own = lax.dynamic_index_in_dim(blocks, index, 0, keepdims=False)

        def slot_tile(slot):
            other = lax.dynamic_index_in_dim(blocks, partner_ids[index, slot], 0, keepdims=False)
            return lax.cond(slot < counts[index], lambda: pair_tile(own, other, table), lambda: jnp.zeros((VEC, VEC), jnp.float32))
        return lax.map(slot_tile, jnp.arange(SLOTS).astype(jnp.int32))
    tiles = lax.map(row_tiles, block_ids)

    def apply(vector):
        picked = vector[partner_ids]
        products = jnp.einsum('nsvw,nsw->nsv', tiles, picked, precision=lax.Precision.HIGHEST)
        return lax.optimization_barrier(jnp.sum(jnp.where(valid[:, :, None], products, 0.0), axis=1))
    first_raw = apply(start)
    first_vec = first_raw / jnp.sqrt(jnp.mean(first_raw * first_raw) + norm_eps)
    second_raw = apply(first_vec)
    second_vec = second_raw / jnp.sqrt(jnp.mean(second_raw * second_raw) + norm_eps)
    return (first_vec, second_vec)
```

```python
import functools
import math

import jax
import jax.numpy as jnp
import numpy as np
from jax import lax
from jax.experimental import pallas as pl
from jax.experimental.pallas import tpu as pltpu
from jax.sharding import PartitionSpec as P

score_gain = 0.4
norm_eps = 1e-06
MESH = pl.DeviceIdType.MESH
HIGHEST = lax.Precision.HIGHEST


def line_order(lines):
    half, quarter = lines // 2, lines // 4
    rows = (quarter + 1 + 7) // 8 * 8
    order = np.zeros((4, rows), np.int32)
    real = np.zeros((4, rows), np.float32)
    base = list(range(1, quarter + 1)) + [0]
    for r in range(rows):
        g = base[r] if r < len(base) else 0
        order[:, r] = [g, half - g, half + g, (lines - g) % lines]
        if r < len(base):
            real[:, r] = 1.0 if 0 < g < quarter else [1.0, 0.0, 1.0, 0.0]
    angle = np.zeros(rows)
    angle[: len(base)] = 2.0 * math.pi * np.array(base) / lines
    return order, real, angle


def constants(lines, width):
    order, real, angle = line_order(lines)
    rows = order.shape[1]
    pick = np.zeros((4 * rows, lines), np.float32)
    pick[np.arange(4 * rows), order.reshape(-1)] = 1.0
    pad = np.zeros((width, lines), np.float32)
    pad[np.arange(lines), np.arange(lines)] = 1.0
    coef = np.stack([np.cos(angle), np.sin(angle), np.cos(2.0 * angle)])
    coef = np.broadcast_to(coef[:, :, None], (3, rows, 128)).astype(np.float32)
    keep = np.broadcast_to(real[:, rows - 8 :, None], (4, 8, 128)).astype(np.float32)
    t = 2.0 * math.pi * np.arange(lines) / lines
    table = np.zeros((2, 8, width), np.float32)
    table[0, 0:3, :lines] = [np.cos(t), np.sin(t), np.cos(2.0 * t)]
    table[1, 3:6, :lines] = table[0, 0:3, :lines]
    table[1, 6, :lines] = 1.0
    return pick, pad, coef, keep, table


def kernel(
    nblk, ncols, lines,
    counts_ref, partners_ref, start_ref, images_ref, pick_ref, pad_ref, coef_ref, keep_ref, table_ref,
    out_ref,
    recv, own, other, s0, s1, s2, s3, left, packet, send_sem, recv_sem, psend_sem, precv_sem,
):
    scores = (s0, s1, s2, s3)
    count = images_ref.shape[0]
    share = count // ncols
    fetch = recv.shape[0]
    halo = fetch // share
    slots = partners_ref.shape[1]
    width = other.shape[0]
    rows = own.shape[1] // 4
    half_images = count // 2
    row = lax.axis_index("rows")
    col = lax.axis_index("cols")
    me = row * ncols + col
    total = nblk * ncols
    ring = nblk == 2 * halo

    sends = []
    for k in range(1, halo + 1):
        for b in range(share):
            f = (k - 1) * share + b
            target = lax.rem(row - k + nblk, nblk)
            copy = pltpu.make_async_remote_copy(
                src_ref=images_ref.at[col * share + b],
                dst_ref=recv.at[f],
                send_sem=send_sem.at[f],
                recv_sem=recv_sem.at[f],
                device_id=(target, col),
                device_id_type=MESH,
            )
            copy.start()
            sends.append(copy)

    left[...] = jnp.zeros_like(left)

    @pl.loop(0, count)
    def _(a):
        own[a] = jnp.dot(
            pick_ref[...], images_ref[a], preferred_element_type=jnp.float32
        ).astype(jnp.bfloat16)

    scale = score_gain * math.log2(math.e)
    lane = lax.broadcasted_iota(jnp.int32, (8, width), 1)
    side = jnp.where(row >= nblk // 2, 1, 0)
    high = jnp.where(col >= ncols // 2, 1, 0)
    mixed = lax.rem(side + high, 2)
    split = fetch - share if ring else fetch
    units = 2 * split + (fetch - split)

    def unit(u, carry):
        f = jnp.where(u < 2 * split, u // 2, u - split)
        h = jnp.where(u < 2 * split, lax.rem(u, 2), mixed)
        fresh = jnp.where(u < 2 * split, 1 - lax.rem(u, 2), 1)

        @pl.when(fresh == 1)
        def _():
            pltpu.make_async_copy(recv.at[f], recv.at[f], recv_sem.at[f]).wait()
            other[...] = jnp.dot(
                pad_ref[...], recv[f], preferred_element_type=jnp.float32
            ).astype(jnp.bfloat16)

        for i in range(half_images):
            s_ref = scores[i]
            a = h * half_images + i
            s = lax.dot_general(
                own[a], other[...], (((1,), (1,)), ((), ())), preferred_element_type=jnp.float32
            )
            s_ref[...] = s
            top = jnp.max(s.reshape(4 * rows // 8, 8, width), axis=0)
            acc = [jnp.zeros((8, width), jnp.float32) for _ in range(4)]
            for g in range(rows // 8):
                w = []
                for j in range(4):
                    part = s_ref[j * rows + g * 8 : j * rows + g * 8 + 8, :]
                    part = jnp.exp2((part - top) * scale)
                    if g == rows // 8 - 1:
                        part = part * keep_ref[j][:, 0:1]
                    w.append(part)
                s14, d14 = w[0] + w[3], w[0] - w[3]
                s23, d23 = w[1] + w[2], w[1] - w[2]
                both = s14 + s23
                at = slice(g * 8, g * 8 + 8)
                acc[0] = acc[0] + (s14 - s23) * coef_ref[0, at, 0:1]
                acc[1] = acc[1] + (d14 + d23) * coef_ref[1, at, 0:1]
                acc[2] = acc[2] + both * coef_ref[2, at, 0:1]
                acc[3] = acc[3] + both
            masked = jnp.where(lane < lines, top, -jnp.inf)
            peak = jnp.max(masked)
            factor = jnp.exp2((masked - peak) * scale)
            for p in range(4):
                left[p, pl.ds(f * count + a, 1), :] = jnp.sum(acc[p] * factor, axis=0, keepdims=True)
        return carry

    lax.fori_loop(0, units, unit, 0)

    npair = fetch * count
    nt = (((1,), (1,)), ((), ()))
    first = lax.dot_general(
        table_ref[0], left[0:2].reshape(2 * npair, width), nt, precision=HIGHEST,
        preferred_element_type=jnp.float32,
    )
    second = lax.dot_general(
        table_ref[1], left[2:4].reshape(2 * npair, width), nt, precision=HIGHEST,
        preferred_element_type=jnp.float32,
    )
    sums = second[6:7, npair:]
    sums = jnp.concatenate([sums, sums], axis=1)
    inverse = jnp.where(sums > 0.0, 1.0 / sums, 0.0)
    prow = lax.broadcasted_iota(jnp.int32, (8, 2 * npair), 0)
    plane = lax.broadcasted_iota(jnp.int32, (8, 2 * npair), 1)
    value = jnp.where(prow < 3, first, jnp.where(prow < 6, second, 0.0)) * inverse
    valid = jnp.zeros((8, 2 * npair), jnp.float32)
    for s in range(slots):
        on = jnp.where(counts_ref[0] > s, 1.0, 0.0)
        valid = valid + jnp.where(plane == partners_ref[0, s], on, 0.0)
    packet[...] = jnp.where(prow == 6, valid, value)
    packet[7:8, :] = jnp.zeros((1, 2 * npair), jnp.float32)
    packet[7:8, 0 : start_ref.shape[1]] = start_ref[...]
    out_ref[me] = packet[...]

    def give(t, carry):
        target = lax.rem(me + t, total)
        pltpu.make_async_remote_copy(
            src_ref=packet,
            dst_ref=out_ref.at[me],
            send_sem=psend_sem,
            recv_sem=precv_sem,
            device_id=(target // ncols, lax.rem(target, ncols)),
            device_id_type=MESH,
        ).start()
        return carry

    lax.fori_loop(1, total, give, 0)
    for copy in sends:
        copy.wait_send()
    everyone = out_ref.at[pl.ds(0, total - 1)]
    pltpu.make_async_copy(everyone, everyone, psend_sem).wait()
    pltpu.make_async_copy(everyone, everyone, precv_sem).wait()


def body(images, partners, counts, start):
    count, lines, radii = images.shape
    slots = partners.shape[1]
    halo = slots // 2
    ncols = lax.axis_size("cols")
    nblk = lax.axis_size("rows")
    share = count // ncols
    width = (lines + 127) // 128 * 128
    pick, pad, coef, keep, table = constants(lines, width)
    rows4 = pick.shape[0]
    total = nblk * ncols
    npair = halo * share * count
    vmem = pl.BlockSpec(memory_space=pltpu.VMEM)
    smem = pl.BlockSpec(memory_space=pltpu.SMEM)
    packets = pl.pallas_call(
        functools.partial(kernel, nblk, ncols, lines),
        out_shape=jax.ShapeDtypeStruct((total, 8, 2 * npair), jnp.float32),
        in_specs=[smem, smem] + [vmem] * 7,
        out_specs=vmem,
        scratch_shapes=[
            pltpu.VMEM((halo * share, lines, radii), jnp.bfloat16),
            pltpu.VMEM((count, rows4, radii), jnp.bfloat16),
            pltpu.VMEM((width, radii), jnp.bfloat16),
            pltpu.VMEM((rows4, width), jnp.float32),
            pltpu.VMEM((rows4, width), jnp.float32),
            pltpu.VMEM((rows4, width), jnp.float32),
            pltpu.VMEM((rows4, width), jnp.float32),
            pltpu.VMEM((4, npair, width), jnp.float32),
            pltpu.VMEM((8, 2 * npair), jnp.float32),
            pltpu.SemaphoreType.DMA((halo * share,)),
            pltpu.SemaphoreType.DMA((halo * share,)),
            pltpu.SemaphoreType.DMA,
            pltpu.SemaphoreType.DMA,
        ],
        compiler_params=pltpu.CompilerParams(has_side_effects=True, vmem_limit_bytes=40 * 2**20),
    )(
        counts, partners, start, images,
        jnp.asarray(pick, jnp.bfloat16), jnp.asarray(pad, jnp.bfloat16),
        jnp.asarray(coef), jnp.asarray(keep), jnp.asarray(table),
    )

    rel = jnp.stack(
        [packets[:, 0:3, :npair], packets[:, 0:3, npair:], packets[:, 3:6, :npair]], axis=1
    ).reshape(nblk, ncols, 3, 3, halo, share, count)
    chosen = packets[::ncols, 6, :slots]
    ahead = chosen[:, halo:]
    behind = chosen[:, :halo][:, ::-1]
    if nblk == 2 * halo:
        ahead = ahead.at[:, -1].add(chosen[:, 0])
        behind = behind.at[:, -1].add(chosen[:, -1])
    vector = packets[::ncols, 7, : 3 * count].reshape(nblk, 3, count)

    def apply(x):
        split = x.reshape(nblk, 3, ncols, share)
        near = jnp.stack([jnp.roll(split, -k, axis=0) for k in range(1, halo + 1)], axis=1)
        near = near * ahead[:, :, None, None, None]
        forward = jnp.einsum("icpqkba,ikqcb->ipa", rel, near, precision=HIGHEST)
        back = jnp.einsum("icpqkba,ipa->ikqcb", rel, x, precision=HIGHEST)
        result = forward
        for k in range(1, halo + 1):
            term = jnp.roll(back[:, k - 1], k, axis=0) * behind[:, k - 1][:, None, None, None]
            result = result + term.reshape(nblk, 3, count)
        return result

    def normalize(raw):
        return raw / jnp.sqrt(jnp.mean(raw * raw) + norm_eps)

    one = normalize(apply(vector))
    two = normalize(apply(one))
    row = lax.axis_index("rows")

    def mine(x):
        return lax.dynamic_slice_in_dim(x.reshape(nblk, 3 * count), row, 1, 0)

    return mine(one), mine(two)


def solution(mesh):
    in_specs = (P("rows", None, None), P("rows", None), P("rows"), P("rows", None))
    out_specs = (P("rows", None), P("rows", None))
    return jax.shard_map(body, mesh=mesh, in_specs=in_specs, out_specs=out_specs, check_vma=False)
```

```python
import functools
import math

import jax
import jax.numpy as jnp
import numpy as np
from jax import lax
from jax.experimental import pallas as pl
from jax.experimental.pallas import tpu as pltpu
from jax.sharding import PartitionSpec as P

score_gain = 0.4
norm_eps = 1e-06
MESH = pl.DeviceIdType.MESH
HIGHEST = lax.Precision.HIGHEST


def line_order(lines):
    half, quarter = lines // 2, lines // 4
    rows = (quarter + 1 + 7) // 8 * 8
    order = np.zeros((4, rows), np.int32)
    real = np.zeros((4, rows), np.float32)
    base = list(range(1, quarter + 1)) + [0]
    for r in range(rows):
        g = base[r] if r < len(base) else 0
        order[:, r] = [g, half - g, half + g, (lines - g) % lines]
        if r < len(base):
            real[:, r] = 1.0 if 0 < g < quarter else [1.0, 0.0, 1.0, 0.0]
    angle = np.zeros(rows)
    angle[: len(base)] = 2.0 * math.pi * np.array(base) / lines
    return order, real, angle


def constants(lines, width):
    order, real, angle = line_order(lines)
    rows = order.shape[1]
    coef = np.stack([np.cos(angle), np.sin(angle), np.cos(2.0 * angle)])
    coef = np.broadcast_to(coef[:, :, None], (3, rows, 128)).reshape(-1, 128)
    keep = np.broadcast_to(real[:, rows - 8 :, None], (4, 8, 128)).reshape(-1, 128)
    t = 2.0 * math.pi * np.arange(lines) / lines
    table = np.zeros((2, 8, width), np.float32)
    table[0, 0:3, :lines] = [np.cos(t), np.sin(t), np.cos(2.0 * t)]
    table[1, 3:6, :lines] = table[0, 0:3, :lines]
    table[1, 6, :lines] = 1.0
    pick = np.broadcast_to(order.reshape(-1)[:, None], (4 * rows, 128))
    return np.concatenate([coef, keep, table.reshape(-1, 128), pick]).astype(np.float32)


def iota(shape, axis):
    return lax.broadcasted_iota(jnp.int32, shape, axis)


def onehot(condition, dtype=jnp.float32):
    return jnp.where(condition, 1.0, 0.0).astype(dtype)


def product(left, right):
    return jnp.dot(left, right, precision=HIGHEST, preferred_element_type=jnp.float32)


def product_nt(left, right):
    return lax.dot_general(
        left, right, (((1,), (1,)), ((), ())), precision=HIGHEST, preferred_element_type=jnp.float32
    )


def iterate(gathered, nblk, ncols, halo, share, count, slots):
    total = nblk * ncols
    ring = nblk == 2 * halo
    npair = halo * share * count
    lanes = 2 * npair
    entries = 3 * count
    picks = [gathered[:, q, :] for q in range(8)]
    zero = onehot(iota((nblk, total), 1) == iota((nblk, total), 0) * ncols)
    chosen = product(zero, picks[6])
    start = product(zero, picks[7])
    at = iota((1, lanes), 1)
    at_k = (at % npair) // (share * count)
    place = (halo + 1) * total
    k = iota((place, nblk), 0) // total
    block = iota((place, nblk), 0) % total // ncols
    step = jnp.where(k < halo, k + 1, 0)
    spread = onehot(iota((place, nblk), 1) == (block + step) % nblk)
    entry = iota((total, 128), 1)
    owner = iota((total, 128), 0) % ncols
    mine = onehot((entry < entries) & (entry % count // share == owner))
    r, c = iota((128, 3 * lanes), 0), iota((128, 3 * lanes), 1)
    far = onehot(
        (r < entries) & (r // count == c // lanes) & (r % share == c % lanes % (share * count) // count)
    )
    r, c = iota((128, 2 * lanes), 0), iota((128, 2 * lanes), 1)
    part = c // npair
    near = onehot((r < entries) & (r % count == c % count) & (r // count == part))
    code, k2 = iota((128, lanes), 0), iota((128, lanes), 1) % npair // (share * count)
    ahead = code == halo + k2
    behind = code == halo - 1 - k2
    if ring:
        ahead = ahead | ((code == 0) & (k2 == halo - 1))
        behind = behind | ((code == slots - 1) & (k2 == halo - 1))
    here = product(spread[halo * total :], chosen)
    weight_near = product(here, onehot(ahead))
    others = product(product(spread[: halo * total], chosen), onehot(behind))
    weight_far = jnp.zeros((total, lanes), jnp.float32)
    for d in range(halo):
        weight_far = weight_far + jnp.where(at_k == d, others[d * total : (d + 1) * total], 0.0)

    def apply(x):
        rows = product(spread, x)
        expanded = product(
            jnp.concatenate([rows[d * total : (d + 1) * total] * mine for d in range(halo)], axis=0), far
        )
        own = product(rows[halo * total :], near)
        first, second = jnp.zeros((total, lanes), jnp.float32), jnp.zeros((total, lanes), jnp.float32)
        back = []
        for q in range(3):
            other = jnp.zeros((total, lanes), jnp.float32)
            for d in range(halo):
                piece = expanded[d * total : (d + 1) * total, q * lanes : (q + 1) * lanes]
                other = other + jnp.where(at_k == d, piece, 0.0)
            first = first + picks[q] * other
            second = second + picks[3 + q] * other
            back.append((picks[q] * own[:, :lanes] + picks[3 + q] * own[:, lanes:]) * weight_far)
        forward = jnp.concatenate([first * weight_near, second * weight_near], axis=1)
        forward = product_nt(forward, near)
        back = jnp.concatenate(back, axis=1)
        at_k3 = jnp.concatenate([at_k] * 3, axis=1)
        back = product_nt(
            jnp.concatenate([jnp.where(at_k3 == d, back, 0.0) for d in range(halo)], axis=0), far
        )
        stacked = [back[d * total : (d + 1) * total] * mine for d in range(halo)] + [forward]
        stacked = jnp.concatenate(stacked, axis=0)
        return lax.dot_general(
            spread, stacked, (((0,), (0,)), ((), ())), precision=HIGHEST,
            preferred_element_type=jnp.float32,
        )

    def normalize(raw):
        mean = jnp.sum(raw * raw) / float(nblk * entries)
        return raw / jnp.sqrt(mean + norm_eps)

    one = normalize(apply(start))
    two = normalize(apply(one))
    return one, two


def kernel(
    nblk, ncols, lines,
    counts_ref, partners_ref, start_ref, images_ref, const_ref,
    one_ref, two_ref,
    recv, images, own, pick, pad, gathered, result, other, s0, s1, s2, s3, left, packet, send_sem, recv_sem, psend_sem, precv_sem, local_sem,
):
    scores = (s0, s1, s2, s3)
    count = images_ref.shape[0]
    share = count // ncols
    fetch = recv.shape[0]
    halo = fetch // share
    slots = partners_ref.shape[1]
    width = other.shape[0]
    rows = own.shape[1] // 4
    half_images = count // 2
    row = lax.axis_index("rows")
    col = lax.axis_index("cols")
    me = row * ncols + col
    total = nblk * ncols
    ring = nblk == 2 * halo

    sends = []
    for k in range(1, halo + 1):
        for b in range(share):
            f = (k - 1) * share + b
            target = lax.rem(row - k + nblk, nblk)
            copy = pltpu.make_async_remote_copy(
                src_ref=images_ref.at[col * share + b],
                dst_ref=recv.at[f],
                send_sem=send_sem.at[f],
                recv_sem=recv_sem.at[f],
                device_id=(target, col),
                device_id_type=MESH,
            )
            copy.start()
            sends.append(copy)

    local = pltpu.make_async_copy(images_ref, images, local_sem)
    local.start()
    left[...] = jnp.zeros_like(left)
    table_at = 3 * rows + 32
    pick_at = table_at + 16 * width // 128
    order = const_ref[pick_at : pick_at + 4 * rows, :]
    order = jnp.concatenate([order] * (width // 128), axis=1).astype(jnp.int32)[:, :lines]
    pick[...] = onehot(order == iota((4 * rows, lines), 1), jnp.bfloat16)
    pad[...] = onehot(iota((width, lines), 0) == iota((width, lines), 1), jnp.bfloat16)
    local.wait()

    @pl.loop(0, count)
    def _(a):
        own[a] = jnp.dot(pick[...], images[a], preferred_element_type=jnp.float32).astype(jnp.bfloat16)

    def wide(at):
        return jnp.concatenate([const_ref[at : at + 8, :]] * (width // 128), axis=1)

    scale = score_gain * math.log2(math.e)
    lane = lax.broadcasted_iota(jnp.int32, (8, width), 1)
    side = jnp.where(row >= nblk // 2, 1, 0)
    high = jnp.where(col >= ncols // 2, 1, 0)
    mixed = lax.rem(side + high, 2)
    split = fetch - share if ring else fetch
    units = 2 * split + (fetch - split)

    def unit(u, carry):
        f = jnp.where(u < 2 * split, u // 2, u - split)
        h = jnp.where(u < 2 * split, lax.rem(u, 2), mixed)
        fresh = jnp.where(u < 2 * split, 1 - lax.rem(u, 2), 1)

        @pl.when(fresh == 1)
        def _():
            pltpu.make_async_copy(recv.at[f], recv.at[f], recv_sem.at[f]).wait()
            other[...] = jnp.dot(
                pad[...], recv[f], preferred_element_type=jnp.float32
            ).astype(jnp.bfloat16)

        for i in range(half_images):
            s_ref = scores[i]
            a = h * half_images + i
            s = lax.dot_general(
                own[a], other[...], (((1,), (1,)), ((), ())), preferred_element_type=jnp.float32
            )
            s_ref[...] = s
            top = jnp.max(s.reshape(4 * rows // 8, 8, width), axis=0)
            acc = [jnp.zeros((8, width), jnp.float32) for _ in range(4)]
            for g in range(rows // 8):
                w = []
                for j in range(4):
                    part = s_ref[j * rows + g * 8 : j * rows + g * 8 + 8, :]
                    part = jnp.exp2((part - top) * scale)
                    if g == rows // 8 - 1:
                        part = part * wide(3 * rows + 8 * j)
                    w.append(part)
                s14, d14 = w[0] + w[3], w[0] - w[3]
                s23, d23 = w[1] + w[2], w[1] - w[2]
                both = s14 + s23
                acc[0] = acc[0] + (s14 - s23) * wide(0 * rows + g * 8)
                acc[1] = acc[1] + (d14 + d23) * wide(1 * rows + g * 8)
                acc[2] = acc[2] + both * wide(2 * rows + g * 8)
                acc[3] = acc[3] + both
            masked = jnp.where(lane < lines, top, -jnp.inf)
            peak = jnp.max(masked)
            factor = jnp.exp2((masked - peak) * scale)
            for p in range(4):
                left[p, pl.ds(f * count + a, 1), :] = jnp.sum(acc[p] * factor, axis=0, keepdims=True)
        return carry

    lax.fori_loop(0, units, unit, 0)

    npair = fetch * count
    table = const_ref[table_at:pick_at, :].reshape(2, 8, width)
    first = product_nt(table[0], left[0:2].reshape(2 * npair, width))
    second = product_nt(table[1], left[2:4].reshape(2 * npair, width))
    sums = second[6:7, npair:]
    sums = jnp.concatenate([sums, sums], axis=1)
    inverse = jnp.where(sums > 0.0, 1.0 / sums, 0.0)
    prow = lax.broadcasted_iota(jnp.int32, (8, 2 * npair), 0)
    plane = lax.broadcasted_iota(jnp.int32, (8, 2 * npair), 1)
    value = jnp.where(prow < 3, first, jnp.where(prow < 6, second, 0.0)) * inverse
    valid = jnp.zeros((8, 2 * npair), jnp.float32)
    for s in range(slots):
        on = jnp.where(counts_ref[0] > s, 1.0, 0.0)
        valid = valid + jnp.where(plane == partners_ref[0, s], on, 0.0)
    packet[...] = jnp.where(prow == 6, valid, value)
    packet[7:8, :] = jnp.zeros((1, 2 * npair), jnp.float32)
    packet[7:8, 0 : start_ref.shape[1]] = start_ref[...]
    gathered[me] = packet[...]

    def give(t, carry):
        target = lax.rem(me + t, total)
        pltpu.make_async_remote_copy(
            src_ref=packet,
            dst_ref=gathered.at[me],
            send_sem=psend_sem,
            recv_sem=precv_sem,
            device_id=(target // ncols, lax.rem(target, ncols)),
            device_id_type=MESH,
        ).start()
        return carry

    lax.fori_loop(1, total, give, 0)
    for copy in sends:
        copy.wait_send()
    everyone = gathered.at[pl.ds(0, total - 1)]
    pltpu.make_async_copy(everyone, everyone, psend_sem).wait()
    pltpu.make_async_copy(everyone, everyone, precv_sem).wait()

    one, two = iterate(gathered, nblk, ncols, halo, share, count, slots)
    result[0] = one
    result[1] = two
    entries = one_ref.shape[1]
    one_ref[...] = result[0, pl.ds(row, 1), :][:, :entries]
    two_ref[...] = result[1, pl.ds(row, 1), :][:, :entries]


def body(images, partners, counts, start):
    count, lines, radii = images.shape
    slots = partners.shape[1]
    halo = slots // 2
    ncols = lax.axis_size("cols")
    nblk = lax.axis_size("rows")
    share = count // ncols
    width = (lines + 127) // 128 * 128
    const = constants(lines, width)
    rows4 = (lines // 4 + 8) // 8 * 32
    total = nblk * ncols
    npair = halo * share * count
    vmem = pl.BlockSpec(memory_space=pltpu.VMEM)
    smem = pl.BlockSpec(memory_space=pltpu.SMEM)
    hbm = pl.BlockSpec(memory_space=pl.ANY)
    shape = jax.ShapeDtypeStruct((1, 3 * count), jnp.float32)
    return pl.pallas_call(
        functools.partial(kernel, nblk, ncols, lines),
        out_shape=(shape, shape),
        in_specs=[smem, smem, vmem, hbm, vmem],
        out_specs=(vmem, vmem),
        scratch_shapes=[
            pltpu.VMEM((halo * share, lines, radii), jnp.bfloat16),
            pltpu.VMEM((count, lines, radii), jnp.bfloat16),
            pltpu.VMEM((count, rows4, radii), jnp.bfloat16),
            pltpu.VMEM((rows4, lines), jnp.bfloat16),
            pltpu.VMEM((width, lines), jnp.bfloat16),
            pltpu.VMEM((total, 8, 2 * npair), jnp.float32),
            pltpu.VMEM((2, nblk, 128), jnp.float32),
            pltpu.VMEM((width, radii), jnp.bfloat16),
            pltpu.VMEM((rows4, width), jnp.float32),
            pltpu.VMEM((rows4, width), jnp.float32),
            pltpu.VMEM((rows4, width), jnp.float32),
            pltpu.VMEM((rows4, width), jnp.float32),
            pltpu.VMEM((4, npair, width), jnp.float32),
            pltpu.VMEM((8, 2 * npair), jnp.float32),
            pltpu.SemaphoreType.DMA((halo * share,)),
            pltpu.SemaphoreType.DMA((halo * share,)),
            pltpu.SemaphoreType.DMA,
            pltpu.SemaphoreType.DMA,
            pltpu.SemaphoreType.DMA,
        ],
        compiler_params=pltpu.CompilerParams(has_side_effects=True, vmem_limit_bytes=48 * 2**20),
    )(counts, partners, start, images, jnp.asarray(const))


def solution(mesh):
    in_specs = (P("rows", None, None), P("rows", None), P("rows"), P("rows", None))
    out_specs = (P("rows", None), P("rows", None))
    return jax.shard_map(body, mesh=mesh, in_specs=in_specs, out_specs=out_specs, check_vma=False)
```

```python
import functools
import math

import jax
import jax.numpy as jnp
import numpy as np
from jax import lax
from jax.experimental import pallas as pl
from jax.experimental.pallas import tpu as pltpu
from jax.sharding import PartitionSpec as P

score_gain = 0.4
norm_eps = 1e-06
MESH = pl.DeviceIdType.MESH
HIGHEST = lax.Precision.HIGHEST


def line_order(lines):
    half, quarter = lines // 2, lines // 4
    rows = (quarter + 1 + 7) // 8 * 8
    order = np.zeros((4, rows), np.int32)
    real = np.zeros((4, rows), np.float32)
    base = list(range(1, quarter + 1)) + [0]
    for r in range(rows):
        g = base[r] if r < len(base) else 0
        order[:, r] = [g, half - g, half + g, (lines - g) % lines]
        if r < len(base):
            real[:, r] = 1.0 if 0 < g < quarter else [1.0, 0.0, 1.0, 0.0]
    angle = np.zeros(rows)
    angle[: len(base)] = 2.0 * math.pi * np.array(base) / lines
    return order, real, angle


def constants(lines, width):
    order, real, angle = line_order(lines)
    rows = order.shape[1]
    coef = np.stack([np.cos(angle), np.sin(angle), np.cos(2.0 * angle)])
    coef = np.broadcast_to(coef[:, :, None], (3, rows, 128)).reshape(-1, 128)
    keep = np.broadcast_to(real[:, rows - 8 :, None], (4, 8, 128)).reshape(-1, 128)
    t = 2.0 * math.pi * np.arange(lines) / lines
    table = np.zeros((2, 8, width), np.float32)
    table[0, 0:3, :lines] = [np.cos(t), np.sin(t), np.cos(2.0 * t)]
    table[1, 3:6, :lines] = table[0, 0:3, :lines]
    table[1, 6, :lines] = 1.0
    pick = np.broadcast_to(order.reshape(-1)[:, None], (4 * rows, 128))
    return np.concatenate([coef, keep, table.reshape(-1, 128), pick]).astype(np.float32)


def iota(shape, axis):
    return lax.broadcasted_iota(jnp.int32, shape, axis)


def onehot(condition, dtype=jnp.float32):
    return jnp.where(condition, 1.0, 0.0).astype(dtype)


def product(left, right):
    return jnp.dot(left, right, precision=HIGHEST, preferred_element_type=jnp.float32)


def product_nt(left, right):
    return lax.dot_general(
        left, right, (((1,), (1,)), ((), ())), precision=HIGHEST, preferred_element_type=jnp.float32
    )


def ahead_of(block, step, nblk, halo):
    if nblk != 2 * halo:
        return (block + step + nblk) % nblk
    half = nblk // 2
    place = (block % 2 * half + block // 2 + step + nblk) % nblk
    return place % half * 2 + place // half


def iterate(gathered, nblk, ncols, halo, share, count):
    total = nblk * ncols
    npair = halo * share * count
    lanes = 2 * npair
    entries = 3 * count
    picks = [gathered[:, q, :] for q in range(8)]
    zero = onehot(iota((nblk, total), 1) == iota((nblk, total), 0) * ncols)
    chosen = product(zero, picks[6])
    start = product(zero, picks[7])
    at = iota((1, lanes), 1)
    at_k = (at % npair) // (share * count)
    place = (halo + 1) * total
    k = iota((place, nblk), 0) // total
    block = iota((place, nblk), 0) % total // ncols
    step = jnp.where(k < halo, k + 1, 0)
    spread = onehot(iota((place, nblk), 1) == ahead_of(block, step, nblk, halo))
    entry = iota((total, 128), 1)
    owner = iota((total, 128), 0) % ncols
    mine = onehot((entry < entries) & (entry % count // share == owner))
    r, c = iota((128, 3 * lanes), 0), iota((128, 3 * lanes), 1)
    far = onehot(
        (r < entries) & (r // count == c // lanes) & (r % share == c % lanes % (share * count) // count)
    )
    r, c = iota((128, 2 * lanes), 0), iota((128, 2 * lanes), 1)
    part = c // npair
    near = onehot((r < entries) & (r % count == c % count) & (r // count == part))
    here = product(spread[halo * total :], chosen)
    others = product(spread[: halo * total], chosen)
    home = iota((total, 128), 0) // ncols
    back_home = onehot(entry == home)
    weight_near = jnp.zeros((total, lanes), jnp.float32)
    weight_far = jnp.zeros((total, lanes), jnp.float32)
    for d in range(halo):
        there = onehot(entry == ahead_of(home, d + 1, nblk, halo))
        given = jnp.sum(here * there, axis=1, keepdims=True)
        taken = jnp.sum(others[d * total : (d + 1) * total] * back_home, axis=1, keepdims=True)
        weight_near = weight_near + jnp.where(at_k == d, given, 0.0)
        weight_far = weight_far + jnp.where(at_k == d, taken, 0.0)

    def apply(x):
        rows = product(spread, x)
        expanded = product(
            jnp.concatenate([rows[d * total : (d + 1) * total] * mine for d in range(halo)], axis=0), far
        )
        own = product(rows[halo * total :], near)
        first, second = jnp.zeros((total, lanes), jnp.float32), jnp.zeros((total, lanes), jnp.float32)
        back = []
        for q in range(3):
            other = jnp.zeros((total, lanes), jnp.float32)
            for d in range(halo):
                piece = expanded[d * total : (d + 1) * total, q * lanes : (q + 1) * lanes]
                other = other + jnp.where(at_k == d, piece, 0.0)
            first = first + picks[q] * other
            second = second + picks[3 + q] * other
            back.append((picks[q] * own[:, :lanes] + picks[3 + q] * own[:, lanes:]) * weight_far)
        forward = jnp.concatenate([first * weight_near, second * weight_near], axis=1)
        forward = product_nt(forward, near)
        back = jnp.concatenate(back, axis=1)
        at_k3 = jnp.concatenate([at_k] * 3, axis=1)
        back = product_nt(
            jnp.concatenate([jnp.where(at_k3 == d, back, 0.0) for d in range(halo)], axis=0), far
        )
        stacked = [back[d * total : (d + 1) * total] * mine for d in range(halo)] + [forward]
        stacked = jnp.concatenate(stacked, axis=0)
        return lax.dot_general(
            spread, stacked, (((0,), (0,)), ((), ())), precision=HIGHEST,
            preferred_element_type=jnp.float32,
        )

    def normalize(raw):
        mean = jnp.sum(raw * raw) / float(nblk * entries)
        return raw / jnp.sqrt(mean + norm_eps)

    one = normalize(apply(start))
    two = normalize(apply(one))
    return one, two


def kernel(
    nblk, ncols, lines,
    counts_ref, partners_ref, start_ref, images_ref, const_ref,
    one_ref, two_ref,
    recv, images, own, pick, pad, gathered, result, other, s0, s1, s2, s3, left, packet, send_sem, recv_sem, psend_sem, precv_sem, gsend_sem, grecv_sem, local_sem,
):
    scores = (s0, s1, s2, s3)
    count = images_ref.shape[0]
    share = count // ncols
    fetch = recv.shape[0]
    halo = fetch // share
    slots = partners_ref.shape[1]
    width = other.shape[0]
    rows = own.shape[1] // 4
    half_images = count // 2
    row = lax.axis_index("rows")
    col = lax.axis_index("cols")
    me = row * ncols + col
    total = nblk * ncols
    ring = nblk == 2 * halo

    sends = []
    for k in range(1, halo + 1):
        for b in range(share):
            f = (k - 1) * share + b
            target = ahead_of(row, -k, nblk, halo)
            copy = pltpu.make_async_remote_copy(
                src_ref=images_ref.at[col * share + b],
                dst_ref=recv.at[f],
                send_sem=send_sem.at[f],
                recv_sem=recv_sem.at[f],
                device_id=(target, col),
                device_id_type=MESH,
            )
            copy.start()
            sends.append(copy)

    local = pltpu.make_async_copy(images_ref, images, local_sem)
    local.start()
    left[...] = jnp.zeros_like(left)
    table_at = 3 * rows + 32
    pick_at = table_at + 16 * width // 128
    order = const_ref[pick_at : pick_at + 4 * rows, :]
    order = jnp.concatenate([order] * (width // 128), axis=1).astype(jnp.int32)[:, :lines]
    pick[...] = onehot(order == iota((4 * rows, lines), 1), jnp.bfloat16)
    pad[...] = onehot(iota((width, lines), 0) == iota((width, lines), 1), jnp.bfloat16)
    local.wait()

    @pl.loop(0, count)
    def _(a):
        own[a] = jnp.dot(pick[...], images[a], preferred_element_type=jnp.float32).astype(jnp.bfloat16)

    def wide(at):
        return jnp.concatenate([const_ref[at : at + 8, :]] * (width // 128), axis=1)

    scale = score_gain * math.log2(math.e)
    lane = lax.broadcasted_iota(jnp.int32, (8, width), 1)
    side = lax.rem(row, 2)
    high = jnp.where(col >= ncols // 2, 1, 0)
    mixed = lax.rem(side + high, 2)
    split = fetch - share if ring else fetch
    units = 2 * split + (fetch - split)

    def unit(u, carry):
        f = jnp.where(u < 2 * split, u // 2, u - split)
        h = jnp.where(u < 2 * split, lax.rem(u, 2), mixed)
        fresh = jnp.where(u < 2 * split, 1 - lax.rem(u, 2), 1)

        @pl.when(fresh == 1)
        def _():
            pltpu.make_async_copy(recv.at[f], recv.at[f], recv_sem.at[f]).wait()
            other[...] = jnp.dot(
                pad[...], recv[f], preferred_element_type=jnp.float32
            ).astype(jnp.bfloat16)

        for i in range(half_images):
            s_ref = scores[i]
            a = h * half_images + i
            s = lax.dot_general(
                own[a], other[...], (((1,), (1,)), ((), ())), preferred_element_type=jnp.float32
            )
            s_ref[...] = s
            top = jnp.max(s.reshape(4 * rows // 8, 8, width), axis=0)
            acc = [jnp.zeros((8, width), jnp.float32) for _ in range(4)]
            for g in range(rows // 8):
                w = []
                for j in range(4):
                    part = s_ref[j * rows + g * 8 : j * rows + g * 8 + 8, :]
                    part = jnp.exp2((part - top) * scale)
                    if g == rows // 8 - 1:
                        part = part * wide(3 * rows + 8 * j)
                    w.append(part)
                s14, d14 = w[0] + w[3], w[0] - w[3]
                s23, d23 = w[1] + w[2], w[1] - w[2]
                both = s14 + s23
                acc[0] = acc[0] + (s14 - s23) * wide(0 * rows + g * 8)
                acc[1] = acc[1] + (d14 + d23) * wide(1 * rows + g * 8)
                acc[2] = acc[2] + both * wide(2 * rows + g * 8)
                acc[3] = acc[3] + both
            masked = jnp.where(lane < lines, top, -jnp.inf)
            peak = jnp.max(masked)
            factor = jnp.exp2((masked - peak) * scale)
            for p in range(4):
                left[p, pl.ds(f * count + a, 1), :] = jnp.sum(acc[p] * factor, axis=0, keepdims=True)
        return carry

    lax.fori_loop(0, units, unit, 0)

    npair = fetch * count
    table = const_ref[table_at:pick_at, :].reshape(2, 8, width)
    first = product_nt(table[0], left[0:2].reshape(2 * npair, width))
    second = product_nt(table[1], left[2:4].reshape(2 * npair, width))
    sums = second[6:7, npair:]
    sums = jnp.concatenate([sums, sums], axis=1)
    inverse = jnp.where(sums > 0.0, 1.0 / sums, 0.0)
    prow = lax.broadcasted_iota(jnp.int32, (8, 2 * npair), 0)
    plane = lax.broadcasted_iota(jnp.int32, (8, 2 * npair), 1)
    value = jnp.where(prow < 3, first, jnp.where(prow < 6, second, 0.0)) * inverse
    valid = jnp.zeros((8, 2 * npair), jnp.float32)
    for s in range(slots):
        on = jnp.where(counts_ref[0] > s, 1.0, 0.0)
        code = partners_ref[0, s]
        offset = jnp.where(code < halo, code - halo, code - halo + 1)
        valid = valid + jnp.where(plane == lax.rem(row + offset + nblk, nblk), on, 0.0)
    packet[...] = jnp.where(prow == 6, valid, value)
    packet[7:8, :] = jnp.zeros((1, 2 * npair), jnp.float32)
    packet[7:8, 0 : start_ref.shape[1]] = start_ref[...]
    gathered[me] = packet[...]

    def give(source, target, device, send, recv):
        pltpu.make_async_remote_copy(
            src_ref=source, dst_ref=target, send_sem=send, recv_sem=recv,
            device_id=device, device_id_type=MESH,
        ).start()

    def settle(size, sem):
        some = gathered.at[pl.ds(0, size)]
        pltpu.make_async_copy(some, some, sem).wait()

    for t in range(1, ncols):
        give(packet, gathered.at[me], (row, lax.rem(col + t, ncols)), psend_sem, precv_sem)
    settle(ncols - 1, precv_sem)
    group = gathered.at[pl.ds(row * ncols, ncols)]

    def give_row(t, carry):
        give(group, group, (lax.rem(row + t, nblk), col), gsend_sem, grecv_sem)
        return carry

    lax.fori_loop(1, nblk, give_row, 0)
    for copy in sends:
        copy.wait_send()
    settle(ncols - 1, psend_sem)
    settle((nblk - 1) * ncols, gsend_sem)
    settle((nblk - 1) * ncols, grecv_sem)

    one, two = iterate(gathered, nblk, ncols, halo, share, count)
    result[0] = one
    result[1] = two
    entries = one_ref.shape[1]
    one_ref[...] = result[0, pl.ds(row, 1), :][:, :entries]
    two_ref[...] = result[1, pl.ds(row, 1), :][:, :entries]


def body(images, partners, counts, start):
    count, lines, radii = images.shape
    slots = partners.shape[1]
    halo = slots // 2
    ncols = lax.axis_size("cols")
    nblk = lax.axis_size("rows")
    share = count // ncols
    width = (lines + 127) // 128 * 128
    const = constants(lines, width)
    rows4 = (lines // 4 + 8) // 8 * 32
    total = nblk * ncols
    npair = halo * share * count
    vmem = pl.BlockSpec(memory_space=pltpu.VMEM)
    smem = pl.BlockSpec(memory_space=pltpu.SMEM)
    hbm = pl.BlockSpec(memory_space=pl.ANY)
    shape = jax.ShapeDtypeStruct((1, 3 * count), jnp.float32)
    return pl.pallas_call(
        functools.partial(kernel, nblk, ncols, lines),
        out_shape=(shape, shape),
        in_specs=[smem, smem, vmem, hbm, vmem],
        out_specs=(vmem, vmem),
        scratch_shapes=[
            pltpu.VMEM((halo * share, lines, radii), jnp.bfloat16),
            pltpu.VMEM((count, lines, radii), jnp.bfloat16),
            pltpu.VMEM((count, rows4, radii), jnp.bfloat16),
            pltpu.VMEM((rows4, lines), jnp.bfloat16),
            pltpu.VMEM((width, lines), jnp.bfloat16),
            pltpu.VMEM((total, 8, 2 * npair), jnp.float32),
            pltpu.VMEM((2, nblk, 128), jnp.float32),
            pltpu.VMEM((width, radii), jnp.bfloat16),
            pltpu.VMEM((rows4, width), jnp.float32),
            pltpu.VMEM((rows4, width), jnp.float32),
            pltpu.VMEM((rows4, width), jnp.float32),
            pltpu.VMEM((rows4, width), jnp.float32),
            pltpu.VMEM((4, npair, width), jnp.float32),
            pltpu.VMEM((8, 2 * npair), jnp.float32),
            pltpu.SemaphoreType.DMA((halo * share,)),
            pltpu.SemaphoreType.DMA((halo * share,)),
            pltpu.SemaphoreType.DMA,
            pltpu.SemaphoreType.DMA,
            pltpu.SemaphoreType.DMA,
            pltpu.SemaphoreType.DMA,
            pltpu.SemaphoreType.DMA,
        ],
        compiler_params=pltpu.CompilerParams(has_side_effects=True, vmem_limit_bytes=48 * 2**20),
    )(counts, partners, start, images, jnp.asarray(const))


def solution(mesh):
    in_specs = (P("rows", None, None), P("rows", None), P("rows"), P("rows", None))
    out_specs = (P("rows", None), P("rows", None))
    return jax.shard_map(body, mesh=mesh, in_specs=in_specs, out_specs=out_specs, check_vma=False)
```

```python
import functools
import math

import jax
import jax.numpy as jnp
import numpy as np
from jax import lax
from jax.experimental import pallas as pl
from jax.experimental.pallas import tpu as pltpu
from jax.sharding import PartitionSpec as P

score_gain = 0.4
norm_eps = 1e-06
MESH = pl.DeviceIdType.MESH
HIGHEST = lax.Precision.HIGHEST


def line_order(lines):
    half, quarter = lines // 2, lines // 4
    rows = (quarter + 1 + 7) // 8 * 8
    order = np.zeros((4, rows), np.int32)
    real = np.zeros((4, rows), np.float32)
    base = list(range(1, quarter + 1)) + [0]
    for r in range(rows):
        g = base[r] if r < len(base) else 0
        order[:, r] = [g, half - g, half + g, (lines - g) % lines]
        if r < len(base):
            real[:, r] = 1.0 if 0 < g < quarter else [1.0, 0.0, 1.0, 0.0]
    angle = np.zeros(rows)
    angle[: len(base)] = 2.0 * math.pi * np.array(base) / lines
    return order, real, angle


def constants(lines, width):
    order, real, angle = line_order(lines)
    rows = order.shape[1]
    coef = np.stack([np.cos(angle), np.sin(angle), np.cos(2.0 * angle)])
    coef = np.broadcast_to(coef[:, :, None], (3, rows, 128)).reshape(-1, 128)
    keep = np.broadcast_to(real[:, rows - 8 :, None], (4, 8, 128)).reshape(-1, 128)
    t = 2.0 * math.pi * np.arange(lines) / lines
    table = np.zeros((2, 8, width), np.float32)
    table[0, 0:3, :lines] = [np.cos(t), np.sin(t), np.cos(2.0 * t)]
    table[1, 3:6, :lines] = table[0, 0:3, :lines]
    table[1, 6, :lines] = 1.0
    pick = np.broadcast_to(order.reshape(-1)[:, None], (4 * rows, 128))
    return np.concatenate([coef, keep, table.reshape(-1, 128), pick]).astype(np.float32)


def iota(shape, axis):
    return lax.broadcasted_iota(jnp.int32, shape, axis)


def onehot(condition, dtype=jnp.float32):
    return jnp.where(condition, 1.0, 0.0).astype(dtype)


def product(left, right):
    return jnp.dot(left, right, precision=HIGHEST, preferred_element_type=jnp.float32)


def product_nt(left, right):
    return lax.dot_general(
        left, right, (((1,), (1,)), ((), ())), precision=HIGHEST, preferred_element_type=jnp.float32
    )


def iterate(gathered, nblk, ncols, halo, share, count, slots):
    total = nblk * ncols
    ring = nblk == 2 * halo
    npair = halo * share * count
    lanes = 2 * npair
    entries = 3 * count
    picks = [gathered[:, q, :] for q in range(8)]
    zero = onehot(iota((nblk, total), 1) == iota((nblk, total), 0) * ncols)
    chosen = product(zero, picks[6])
    start = product(zero, picks[7])
    at = iota((1, lanes), 1)
    at_k = (at % npair) // (share * count)
    place = (halo + 1) * total
    k = iota((place, nblk), 0) // total
    block = iota((place, nblk), 0) % total // ncols
    step = jnp.where(k < halo, k + 1, 0)
    spread = onehot(iota((place, nblk), 1) == (block + step) % nblk)
    entry = iota((total, 128), 1)
    owner = iota((total, 128), 0) % ncols
    mine = onehot((entry < entries) & (entry % count // share == owner))
    r, c = iota((128, 3 * lanes), 0), iota((128, 3 * lanes), 1)
    far = onehot(
        (r < entries) & (r // count == c // lanes) & (r % share == c % lanes % (share * count) // count)
    )
    r, c = iota((128, 2 * lanes), 0), iota((128, 2 * lanes), 1)
    part = c // npair
    near = onehot((r < entries) & (r % count == c % count) & (r // count == part))
    code, k2 = iota((128, lanes), 0), iota((128, lanes), 1) % npair // (share * count)
    ahead = code == halo + k2
    behind = code == halo - 1 - k2
    if ring:
        ahead = ahead | ((code == 0) & (k2 == halo - 1))
        behind = behind | ((code == slots - 1) & (k2 == halo - 1))
    here = product(spread[halo * total :], chosen)
    weight_near = product(here, onehot(ahead))
    others = product(product(spread[: halo * total], chosen), onehot(behind))
    weight_far = jnp.zeros((total, lanes), jnp.float32)
    for d in range(halo):
        weight_far = weight_far + jnp.where(at_k == d, others[d * total : (d + 1) * total], 0.0)

    def apply(x):
        rows = product(spread, x)
        expanded = product(
            jnp.concatenate([rows[d * total : (d + 1) * total] * mine for d in range(halo)], axis=0), far
        )
        own = product(rows[halo * total :], near)
        first, second = jnp.zeros((total, lanes), jnp.float32), jnp.zeros((total, lanes), jnp.float32)
        back = []
        for q in range(3):
            other = jnp.zeros((total, lanes), jnp.float32)
            for d in range(halo):
                piece = expanded[d * total : (d + 1) * total, q * lanes : (q + 1) * lanes]
                other = other + jnp.where(at_k == d, piece, 0.0)
            first = first + picks[q] * other
            second = second + picks[3 + q] * other
            back.append((picks[q] * own[:, :lanes] + picks[3 + q] * own[:, lanes:]) * weight_far)
        forward = jnp.concatenate([first * weight_near, second * weight_near], axis=1)
        forward = product_nt(forward, near)
        back = jnp.concatenate(back, axis=1)
        at_k3 = jnp.concatenate([at_k] * 3, axis=1)
        back = product_nt(
            jnp.concatenate([jnp.where(at_k3 == d, back, 0.0) for d in range(halo)], axis=0), far
        )
        stacked = [back[d * total : (d + 1) * total] * mine for d in range(halo)] + [forward]
        stacked = jnp.concatenate(stacked, axis=0)
        return lax.dot_general(
            spread, stacked, (((0,), (0,)), ((), ())), precision=HIGHEST,
            preferred_element_type=jnp.float32,
        )

    def normalize(raw):
        mean = jnp.sum(raw * raw) / float(nblk * entries)
        return raw / jnp.sqrt(mean + norm_eps)

    one = normalize(apply(start))
    two = normalize(apply(one))
    return one, two


def kernel(
    nblk, ncols, lines,
    counts_ref, partners_ref, start_ref, images_ref, const_ref,
    one_ref, two_ref,
    recv, images, own, pick, pad, gathered, result, other, s0, s1, s2, s3, left, packet, send_sem, recv_sem, psend_sem, precv_sem, gsend_sem, grecv_sem, local_sem,
):
    scores = (s0, s1, s2, s3)
    count = images_ref.shape[0]
    share = count // ncols
    fetch = recv.shape[0]
    halo = fetch // share
    slots = partners_ref.shape[1]
    width = other.shape[0]
    rows = own.shape[1] // 4
    half_images = count // 2
    row = lax.axis_index("rows")
    col = lax.axis_index("cols")
    me = row * ncols + col
    total = nblk * ncols
    ring = nblk == 2 * halo

    sends = []
    for k in range(1, halo + 1):
        for b in range(share):
            f = (k - 1) * share + b
            target = lax.rem(row - k + nblk, nblk)
            copy = pltpu.make_async_remote_copy(
                src_ref=images_ref.at[col * share + b],
                dst_ref=recv.at[f],
                send_sem=send_sem.at[f],
                recv_sem=recv_sem.at[f],
                device_id=(target, col),
                device_id_type=MESH,
            )
            copy.start()
            sends.append(copy)

    local = pltpu.make_async_copy(images_ref, images, local_sem)
    local.start()
    left[...] = jnp.zeros_like(left)
    table_at = 3 * rows + 32
    pick_at = table_at + 16 * width // 128
    order = const_ref[pick_at : pick_at + 4 * rows, :]
    order = jnp.concatenate([order] * (width // 128), axis=1).astype(jnp.int32)[:, :lines]
    pick[...] = onehot(order == iota((4 * rows, lines), 1), jnp.bfloat16)
    pad[...] = onehot(iota((width, lines), 0) == iota((width, lines), 1), jnp.bfloat16)
    local.wait()

    @pl.loop(0, count)
    def _(a):
        own[a] = jnp.dot(pick[...], images[a], preferred_element_type=jnp.float32).astype(jnp.bfloat16)

    def wide(at):
        return jnp.concatenate([const_ref[at : at + 8, :]] * (width // 128), axis=1)

    scale = score_gain * math.log2(math.e)
    lane = lax.broadcasted_iota(jnp.int32, (8, width), 1)
    side = jnp.where(row >= nblk // 2, 1, 0)
    high = jnp.where(col >= ncols // 2, 1, 0)
    mixed = lax.rem(side + high, 2)
    split = fetch - share if ring else fetch
    units = 2 * split + (fetch - split)

    def unit(u, carry):
        f = jnp.where(u < 2 * split, u // 2, u - split)
        h = jnp.where(u < 2 * split, lax.rem(u, 2), mixed)
        fresh = jnp.where(u < 2 * split, 1 - lax.rem(u, 2), 1)

        @pl.when(fresh == 1)
        def _():
            pltpu.make_async_copy(recv.at[f], recv.at[f], recv_sem.at[f]).wait()
            other[...] = jnp.dot(
                pad[...], recv[f], preferred_element_type=jnp.float32
            ).astype(jnp.bfloat16)

        for i in range(half_images):
            s_ref = scores[i]
            a = h * half_images + i
            s = lax.dot_general(
                own[a], other[...], (((1,), (1,)), ((), ())), preferred_element_type=jnp.float32
            )
            s_ref[...] = s
            top = jnp.max(s.reshape(4 * rows // 8, 8, width), axis=0)
            acc = [jnp.zeros((8, width), jnp.float32) for _ in range(4)]
            for g in range(rows // 8):
                w = []
                for j in range(4):
                    part = s_ref[j * rows + g * 8 : j * rows + g * 8 + 8, :]
                    part = jnp.exp2((part - top) * scale)
                    if g == rows // 8 - 1:
                        part = part * wide(3 * rows + 8 * j)
                    w.append(part)
                s14, d14 = w[0] + w[3], w[0] - w[3]
                s23, d23 = w[1] + w[2], w[1] - w[2]
                both = s14 + s23
                acc[0] = acc[0] + (s14 - s23) * wide(0 * rows + g * 8)
                acc[1] = acc[1] + (d14 + d23) * wide(1 * rows + g * 8)
                acc[2] = acc[2] + both * wide(2 * rows + g * 8)
                acc[3] = acc[3] + both
            masked = jnp.where(lane < lines, top, -jnp.inf)
            peak = jnp.max(masked)
            factor = jnp.exp2((masked - peak) * scale)
            for p in range(4):
                left[p, pl.ds(f * count + a, 1), :] = jnp.sum(acc[p] * factor, axis=0, keepdims=True)
        return carry

    lax.fori_loop(0, units, unit, 0)

    npair = fetch * count
    table = const_ref[table_at:pick_at, :].reshape(2, 8, width)
    first = product_nt(table[0], left[0:2].reshape(2 * npair, width))
    second = product_nt(table[1], left[2:4].reshape(2 * npair, width))
    sums = second[6:7, npair:]
    sums = jnp.concatenate([sums, sums], axis=1)
    inverse = jnp.where(sums > 0.0, 1.0 / sums, 0.0)
    prow = lax.broadcasted_iota(jnp.int32, (8, 2 * npair), 0)
    plane = lax.broadcasted_iota(jnp.int32, (8, 2 * npair), 1)
    value = jnp.where(prow < 3, first, jnp.where(prow < 6, second, 0.0)) * inverse
    valid = jnp.zeros((8, 2 * npair), jnp.float32)
    for s in range(slots):
        on = jnp.where(counts_ref[0] > s, 1.0, 0.0)
        valid = valid + jnp.where(plane == partners_ref[0, s], on, 0.0)
    packet[...] = jnp.where(prow == 6, valid, value)
    packet[7:8, :] = jnp.zeros((1, 2 * npair), jnp.float32)
    packet[7:8, 0 : start_ref.shape[1]] = start_ref[...]
    gathered[me] = packet[...]

    def give(source, target, device, send, recv):
        pltpu.make_async_remote_copy(
            src_ref=source, dst_ref=target, send_sem=send, recv_sem=recv,
            device_id=device, device_id_type=MESH,
        ).start()

    def settle(size, sem):
        some = gathered.at[pl.ds(0, size)]
        pltpu.make_async_copy(some, some, sem).wait()

    for t in range(1, ncols):
        give(packet, gathered.at[me], (row, lax.rem(col + t, ncols)), psend_sem, precv_sem)
    settle(ncols - 1, precv_sem)
    group = gathered.at[pl.ds(row * ncols, ncols)]

    def give_row(t, carry):
        give(group, group, (lax.rem(row + t, nblk), col), gsend_sem, grecv_sem)
        return carry

    lax.fori_loop(1, nblk, give_row, 0)
    for copy in sends:
        copy.wait_send()
    settle(ncols - 1, psend_sem)
    settle((nblk - 1) * ncols, gsend_sem)
    settle((nblk - 1) * ncols, grecv_sem)

    one, two = iterate(gathered, nblk, ncols, halo, share, count, slots)
    result[0] = one
    result[1] = two
    entries = one_ref.shape[1]
    one_ref[...] = result[0, pl.ds(row, 1), :][:, :entries]
    two_ref[...] = result[1, pl.ds(row, 1), :][:, :entries]


def body(images, partners, counts, start):
    count, lines, radii = images.shape
    slots = partners.shape[1]
    halo = slots // 2
    ncols = lax.axis_size("cols")
    nblk = lax.axis_size("rows")
    share = count // ncols
    width = (lines + 127) // 128 * 128
    const = constants(lines, width)
    rows4 = (lines // 4 + 8) // 8 * 32
    total = nblk * ncols
    npair = halo * share * count
    vmem = pl.BlockSpec(memory_space=pltpu.VMEM)
    smem = pl.BlockSpec(memory_space=pltpu.SMEM)
    hbm = pl.BlockSpec(memory_space=pl.ANY)
    shape = jax.ShapeDtypeStruct((1, 3 * count), jnp.float32)
    return pl.pallas_call(
        functools.partial(kernel, nblk, ncols, lines),
        out_shape=(shape, shape),
        in_specs=[smem, smem, vmem, hbm, vmem],
        out_specs=(vmem, vmem),
        scratch_shapes=[
            pltpu.VMEM((halo * share, lines, radii), jnp.bfloat16),
            pltpu.VMEM((count, lines, radii), jnp.bfloat16),
            pltpu.VMEM((count, rows4, radii), jnp.bfloat16),
            pltpu.VMEM((rows4, lines), jnp.bfloat16),
            pltpu.VMEM((width, lines), jnp.bfloat16),
            pltpu.VMEM((total, 8, 2 * npair), jnp.float32),
            pltpu.VMEM((2, nblk, 128), jnp.float32),
            pltpu.VMEM((width, radii), jnp.bfloat16),
            pltpu.VMEM((rows4, width), jnp.float32),
            pltpu.VMEM((rows4, width), jnp.float32),
            pltpu.VMEM((rows4, width), jnp.float32),
            pltpu.VMEM((rows4, width), jnp.float32),
            pltpu.VMEM((4, npair, width), jnp.float32),
            pltpu.VMEM((8, 2 * npair), jnp.float32),
            pltpu.SemaphoreType.DMA((halo * share,)),
            pltpu.SemaphoreType.DMA((halo * share,)),
            pltpu.SemaphoreType.DMA,
            pltpu.SemaphoreType.DMA,
            pltpu.SemaphoreType.DMA,
            pltpu.SemaphoreType.DMA,
            pltpu.SemaphoreType.DMA,
        ],
        compiler_params=pltpu.CompilerParams(has_side_effects=True, vmem_limit_bytes=48 * 2**20),
    )(counts, partners, start, images, jnp.asarray(const))


def solution(mesh):
    in_specs = (P("rows", None, None), P("rows", None), P("rows"), P("rows", None))
    out_specs = (P("rows", None), P("rows", None))
    return jax.shard_map(body, mesh=mesh, in_specs=in_specs, out_specs=out_specs, check_vma=False)
```
